32 devices in a mesh: groups: 2 (over x), row: 4 (over y, core), col: 4 (over z).
Axes of the slice: x: 2, y: 2, z: 4, core: 2. Of those that a mesh axis runs over, the one named last changes fastest.
Arguments:
- tokens: bfloat16 [1024, 8192], P(('groups', 'row'), 'col'), parts along dimension 0, may hold values from -6 to 6
- gate_weight: bfloat16 [8192, 16384], P('col', 'row'), may hold values from -0.09375 to 0.09375
- up_weight: bfloat16 [8192, 16384], P('col', 'row'), may hold values from -0.09375 to 0.09375
- down_weight: bfloat16 [16384, 8192], P('row', 'col'), may hold values from -0.09375 to 0.09375
- gate_mask: int32 [64, 128], P('col', 'row'), may hold values from 0 to 1, as said below
- up_mask: int32 [64, 128], P('col', 'row'), may hold values from 0 to 1, as said below
- down_mask: int32 [128, 64], P('row', 'col'), may hold values from 0 to 1, as said below
Outputs:
- mixed: bfloat16 [1024, 8192], P(('groups', 'row'), 'col'), parts along dimension 0
The draws below stay inside these ranges and needn't reach their ends.
There are 2 independent parts, one for each index of `groups`. The reference program is written for one: setup_inputs(seed, part) draws one part's arguments, and reference() takes and returns one part's arrays. A program takes and returns all parts, laid end to end along the dimension named above; an argument that names none is the same for every part. Nothing has to cross between parts.
Inputs may be any that keep to these rules, and one draw needn't show every extreme that they name: `gate_mask`: 1 where a 128 x 128 tile of the gate projection is kept, else 0; the share kept differs from one block of 128 hidden units to another. `up_mask`: 1 where a tile of the up projection is kept, else 0. `down_mask`: 1 where a tile of the down projection is kept, else 0.
All inputs are finite; a program needn't handle non-finite values.
Results may differ from the reference program's by a relative error of at most 0.02.
Values may be sent and summed in bfloat16 or wider, within the bound.
No kernel may reach another device: no remote copies, remote signals or barrier semaphores. Data moves between devices by JAX's collectives and lax.ppermute only.
A program may use at most 256 MiB of HBM per device.

```python
import jax
import jax.numpy as jnp

D = 8192
FF = 16384
TILE = 128
TOKENS = 512
N_ROW = 4
N_COL = 4


def unit_limits(key):
    return jax.random.randint(key, (FF // TILE,), 15, 95)


def draw_gate_mask(key, part):
    limits = unit_limits(key)
    key = jax.random.fold_in(key, 11)
    rolls = jax.random.randint(key, (D // TILE, FF // TILE), 0, 100)
    return (rolls < limits[None, :]).astype(jnp.int32)


def draw_up_mask(key, part):
    limits = unit_limits(key)
    key = jax.random.fold_in(key, 23)
    rolls = jax.random.randint(key, (D // TILE, FF // TILE), 0, 100)
    return (rolls < limits[None, :]).astype(jnp.int32)


def draw_down_mask(key, part):
    limits = unit_limits(key)
    key = jax.random.fold_in(key, 37)
    rolls = jax.random.randint(key, (FF // TILE, D // TILE), 0, 100)
    return (rolls < limits[:, None]).astype(jnp.int32)


def levels(own_key, shape, shards, smallest, top_value):
    def one(dim, blocks):
        draws = jax.random.uniform(jax.random.fold_in(jax.random.fold_in(own_key, 6), dim), (blocks,), jnp.float32, smallest / len(shards), top_value / len(shards))
        return jnp.repeat(jnp.exp(draws), shape[dim] // blocks).reshape((-1,) + (1,) * (len(shape) - dim - 1))

    level = one(*shards[0])
    for cut in shards[1:]:
        level = level * one(*cut)
    return level


def normal_values(stream_key, shape, scale, limit, shards=(), held_as=jnp.bfloat16):
    result = scale * jax.random.normal(stream_key, shape, jnp.float32)
    if shards:
        result = result * levels(stream_key, shape, shards, -0.22, 0.18)
    return jnp.clip(result, -limit, limit).astype(held_as)


def setup_inputs(seed: int = 0, part: int = 0) -> dict:
    streams_of = jax.random.split(jax.random.key(seed), 8)
    part_keys = jax.random.split(jax.random.fold_in(streams_of[7], part), 8)
    tokens = normal_values(part_keys[0], (TOKENS, D), 1.0, 6.0, ((0, 4), (1, 4)))
    gate_weight = normal_values(streams_of[1], (D, FF), (D // 2) ** -0.5, 0.09375, ((0, 4), (1, 4)))
    up_weight = normal_values(streams_of[2], (D, FF), (D // 2) ** -0.5, 0.09375, ((0, 4), (1, 4)))
    down_weight = normal_values(streams_of[3], (FF, D), (FF // 4) ** -0.5, 0.09375, ((0, 4), (1, 4)))
    gate_mask = draw_gate_mask(jax.random.fold_in(streams_of[7], 71), part)
    up_mask = draw_up_mask(jax.random.fold_in(streams_of[7], 71), part)
    down_mask = draw_down_mask(jax.random.fold_in(streams_of[7], 71), part)
    return dict(tokens=tokens, gate_weight=gate_weight, up_weight=up_weight, down_weight=down_weight, gate_mask=gate_mask, up_mask=up_mask, down_mask=down_mask)


def expand(mask):
    return jnp.repeat(jnp.repeat(mask, TILE, axis=0), TILE, axis=1)


def pruned(weight, mask):
    return weight * expand(mask).astype(jnp.bfloat16)


def reference(tokens, gate_weight, up_weight, down_weight, gate_mask, up_mask, down_mask):
    gate_pruned = pruned(gate_weight, gate_mask)
    up_pruned = pruned(up_weight, up_mask)
    down_pruned = pruned(down_weight, down_mask)
    width_block = D // N_COL
    gate = jnp.zeros((TOKENS, FF), jnp.float32)
    up = jnp.zeros((TOKENS, FF), jnp.float32)
    for block in range(N_COL):
        lo = block * width_block
        panel = tokens[:, lo:lo + width_block]
        gate_part = jnp.dot(panel, gate_pruned[lo:lo + width_block], preferred_element_type=jnp.float32)
        up_part = jnp.dot(panel, up_pruned[lo:lo + width_block], preferred_element_type=jnp.float32)
        gate = gate + gate_part.astype(jnp.bfloat16).astype(jnp.float32)
        up = up + up_part.astype(jnp.bfloat16).astype(jnp.float32)
    hidden = (jax.nn.silu(gate) * up).astype(jnp.bfloat16)
    unit_block = FF // N_ROW
    total = jnp.zeros((TOKENS, D), jnp.float32)
    for block in range(N_ROW):
        lo = block * unit_block
        out_part = jnp.dot(hidden[:, lo:lo + unit_block], down_pruned[lo:lo + unit_block], preferred_element_type=jnp.float32)
        total = total + out_part.astype(jnp.bfloat16).astype(jnp.float32)
    return total.astype(jnp.bfloat16)
```

```python
import functools

import jax
import jax.numpy as jnp
from jax import lax
from jax.experimental import pallas as pl
from jax.experimental.pallas import tpu as pltpu
from jax.sharding import PartitionSpec as P

LAG = 2
ANY = pl.BlockSpec(memory_space=pl.ANY)
SMEM = pl.BlockSpec(memory_space=pltpu.SMEM)
VMEM = pl.BlockSpec(memory_space=pltpu.VMEM)
MIB = 1 << 20


def masked(block, mask, row, col, edge):
    strips = []
    for i in range(block.shape[0] // edge):
        tiles = []
        for j in range(block.shape[1] // edge):
            keep = mask[row + i, col + j].astype(jnp.float32).astype(jnp.bfloat16)
            tiles.append(block[i * edge:(i + 1) * edge, j * edge:(j + 1) * edge] * keep)
        strips.append(jnp.concatenate(tiles, axis=1))
    return jnp.concatenate(strips, axis=0)


def partial_kernel(edge, cols, gm, um, tok, x, ga, ua, gb, ub, pa, pb, tok_out, acc):
    k, steps = pl.program_id(0), pl.num_programs(0)
    row = k * (ga.shape[0] // edge)
    units = ga.shape[1]

    @pl.when(k == 0)
    def _():
        acc[...] = jnp.zeros_like(acc)

    for i, (w, m, col) in enumerate(((ga, gm, cols[0]), (ua, um, cols[0]), (gb, gm, cols[1]), (ub, um, cols[1]))):
        acc[:, i * units:(i + 1) * units] += jnp.dot(
            x[...], masked(w, m, row, col, edge), preferred_element_type=jnp.float32
        )

    @pl.when(k == steps - 1)
    def _():
        pa[...] = acc[:, :2 * units].astype(pa.dtype)
        pb[...] = acc[:, 2 * units:].astype(pb.dtype)


def partials(tok, x, gate, up, gm, um, unit, units):
    rows, depth = x.shape
    edge = depth // gm.shape[0]
    block = min(512, depth)
    half = gate.shape[1] // 2 // units
    near = pl.BlockSpec((block, units), lambda k: (k, unit))
    far = pl.BlockSpec((block, units), lambda k: (k, half + unit))
    out = jax.ShapeDtypeStruct((rows, 2 * units), jnp.bfloat16)
    return pl.pallas_call(
        functools.partial(partial_kernel, edge, (unit * units // edge, (half + unit) * units // edge)),
        grid=(depth // block,),
        in_specs=[SMEM, SMEM, ANY, pl.BlockSpec((rows, block), lambda k: (0, k)), near, near, far, far],
        out_specs=[pl.BlockSpec((rows, 2 * units), lambda k: (0, 0))] * 2 + [ANY],
        out_shape=[out, out, jax.ShapeDtypeStruct(tok.shape, tok.dtype)],
        scratch_shapes=[pltpu.VMEM((rows, 4 * units), jnp.float32)],
        input_output_aliases={2: 2},
        compiler_params=pltpu.CompilerParams(vmem_limit_bytes=52 * MIB),
    )(gm, um, tok, x, gate, up, gate, up)


def swiglu(gate, up):
    return gate / (1.0 + jnp.exp(-gate)) * up


def hop_kernel(cols, step, lag, units, wide, sent, z_ref, tok, left_in, right_in, *rest):
    count = sum(len(c) for c in cols)
    own, (left_out, right_out, tok_out, a, b, sems) = rest[:count], rest[count:]
    own_a, own_b = own[:len(cols[0])], own[len(cols[0]):]
    z = z_ref[0]
    n_col = wide[2]
    span = 2 * units

    def each(act):
        for refs, where, to, sem in ((own_a, cols[0], a, 0), (own_b, cols[1], b, 1)):
            for ref, i in zip(refs, where):
                @pl.when(z == i)
                def _(ref=ref, to=to, sem=sem):
                    act(pltpu.make_async_copy(ref, to, sems.at[sem]))

    each(lambda c: c.start())
    if sent[1]:
        at = span if sent[0] else 0
        come = span
        if wide[1]:
            @pl.when(z > 0)
            def _():
                right_out[:, at:at + units] = right_in[:, come:come + units]

            @pl.when(z < n_col - 1)
            def _():
                left_out[:, at:at + units] = left_in[:, come:come + units]
    each(lambda c: c.wait())

    rows = a.shape[0]
    piece = min(16, rows)

    def over(body):
        def one(i, _):
            body(pl.ds(pl.multiple_of(i * piece, piece), piece))
            return 0
        lax.fori_loop(0, rows // piece, one, 0)

    for came, mine, goes, back, origin, end in (
        (left_in, a, left_out, right_out, n_col - 1, 0),
        (right_in, b, right_out, left_out, 0, n_col - 1),
    ):
        if sent[0]:
            @pl.when(z == origin)
            def _(mine=mine, goes=goes):
                goes[:, :span] = mine[...]

            @pl.when((z != origin) & (z != end))
            def _(came=came, mine=mine, goes=goes):
                def add(r):
                    goes[r, :span] = (came[r, :span].astype(jnp.float32) + mine[r, :].astype(jnp.float32)).astype(goes.dtype)
                over(add)
        if sent[1]:
            @pl.when(z == end)
            def _(came=came, mine=mine, back=back):
                def finish(r):
                    total = came[r, :span].astype(jnp.float32) + mine[r, :].astype(jnp.float32)
                    back[r, at:at + units] = swiglu(total[:, :units], total[:, units:]).astype(back.dtype)
                over(finish)


def hop(tok, z, left_in, right_in, own_a, own_b, step, lag, units, arrives, leaves, n_col):
    rows = left_in.shape[0]
    width = (2 * units if leaves[0] else 0) + (units if leaves[1] else 0)
    out = jax.ShapeDtypeStruct((rows, width), jnp.bfloat16)
    cols = (tuple(i for i, _ in own_a), tuple(i for i, _ in own_b))
    return pl.pallas_call(
        functools.partial(hop_kernel, cols, step, lag, units, (*arrives, n_col), leaves),
        in_specs=[SMEM, ANY, VMEM, VMEM] + [ANY] * (len(own_a) + len(own_b)),
        out_specs=[VMEM, VMEM, ANY],
        out_shape=[out, out, jax.ShapeDtypeStruct(tok.shape, tok.dtype)],
        scratch_shapes=[
            pltpu.VMEM((rows, 2 * units), jnp.bfloat16),
            pltpu.VMEM((rows, 2 * units), jnp.bfloat16),
            pltpu.SemaphoreType.DMA((2,)),
        ],
        input_output_aliases={1: 2},
        compiler_params=pltpu.CompilerParams(vmem_limit_bytes=8 * MIB),
    )(z, tok, left_in, right_in, *[x for _, x in own_a], *[x for _, x in own_b])


def project_kernel(picks, edge, units, z_ref, mask, tok, w, *rest):
    hidden, (out, tok_out, held, acc, sem) = rest[:len(picks)], rest[len(picks):]
    k, steps = pl.program_id(0), pl.num_programs(0)
    z = z_ref[0]

    @pl.when(k == 0)
    def _():
        def each(act):
            for ref, (i, slot, at) in zip(hidden, picks):
                @pl.when(z == i)
                def _(ref=ref, slot=slot, at=at):
                    act(pltpu.make_async_copy(ref.at[:, at:at + units], held.at[slot], sem.at[slot]))
        each(lambda c: c.start())
        acc[...] = jnp.zeros_like(acc)
        each(lambda c: c.wait())

    acc[...] += jnp.dot(
        held[k], masked(w, mask, k * (units // edge), 0, edge), preferred_element_type=jnp.float32
    )

    @pl.when(k == steps - 1)
    def _():
        out[...] = acc[...].astype(out.dtype)


def project(tok, z, hidden, down, mask, units):
    rows = hidden[0][3].shape[0]
    depth, width = down.shape
    edge = depth // mask.shape[0]
    slots = depth // units
    return pl.pallas_call(
        functools.partial(project_kernel, tuple(h[:3] for h in hidden), edge, units),
        grid=(slots,),
        in_specs=[SMEM, SMEM, ANY, pl.BlockSpec((units, width), lambda k: (k, 0))] + [ANY] * len(hidden),
        out_specs=[pl.BlockSpec((rows, width), lambda k: (0, 0)), ANY],
        out_shape=[jax.ShapeDtypeStruct((rows, width), jnp.bfloat16), jax.ShapeDtypeStruct(tok.shape, tok.dtype)],
        scratch_shapes=[
            pltpu.VMEM((slots, rows, units), jnp.bfloat16),
            pltpu.VMEM((rows, width), jnp.float32),
            pltpu.SemaphoreType.DMA((slots,)),
        ],
        input_output_aliases={2: 1},
        compiler_params=pltpu.CompilerParams(vmem_limit_bytes=52 * MIB),
    )(z, mask, tok, down, *[h[3] for h in hidden])


def cycle(n_row, n_col):
    def at(r, i):
        return r * n_col + (n_col - 1 - i if r % 2 else i)

    steps = []
    for r in range(n_row):
        mate = r ^ 1 if r ^ 1 < n_row else r
        steps += [(at(r, i), at(r, i + 1)) for i in range(n_col - 1)] + [(at(r, n_col - 1), at(mate, 0))]
    return steps


def shards(n_row, n_col, tokens, gate, up, down, gm, um, dm):
    lag = LAG
    half = gate.shape[1] // 2
    units = min(512, half)
    n_unit = half // units
    xor = n_row & (n_row - 1) == 0
    other = (lambda i, d: i ^ d) if xor else (lambda i, d: (i + d) % n_row)
    order = [0, *range(2, n_row), 1][:n_row]
    n = n_row * n_unit
    z, odd = lax.axis_index("col"), lax.axis_index("row") % 2
    z = jnp.where(odd == 1, n_col - 1 - z, z).astype(jnp.int32).reshape(1)
    to_right = cycle(n_row, n_col)
    to_left = [(j, i) for i, j in to_right]
    tok = jnp.zeros((8, 128), jnp.float32)

    xs = {0: tokens}
    for d in order[1:]:
        xs[d] = lax.ppermute(tokens, "row", [(other(i, d), i) for i in range(n_row)])

    own_a, own_b = [], []
    left_sent, right_sent, left_got, right_got, kind = {}, {}, {}, {}, {}
    outs = {}
    last_sum = n - 1 + lag * (n_col - 2)
    last_end = n - 1 + lag * (n_col - 1)
    last_hop = n - 1 + lag * (2 * n_col - 3)
    first_end = lag * (n_col - 1)

    def place(k):
        t0 = k + first_end
        spots = []
        for i in range(n_col):
            t = t0 + lag * (i - 1)
            buf, what = (right_sent[t0], kind[t0]) if i == 0 else (right_got[t], kind[t])
            spots.append((i, 0, 2 * units if what[0] else 0, buf))
            j = n_col - 1 - i
            buf, what = (left_sent[t0], kind[t0]) if i == 0 else (left_got[t], kind[t])
            spots.append((j, 1, 2 * units if what[0] else 0, buf))
        return spots

    for t in range(last_hop + lag + 1):
        if t < n:
            pa, pb, tok = partials(tok, xs[order[t // n_unit]], gate, up, gm, um, t % n_unit, units)
            own_a.append(pa)
            own_b.append(pb)
        if t <= last_hop:
            kind[t] = (t <= last_sum, t >= first_end)
            if t < lag:
                left_sent[t], right_sent[t] = own_a[t], own_b[t]
            elif t <= last_end:
                mine_a = [(i, own_a[t - lag * (n_col - 1 - i)]) for i in range(n_col) if 0 <= t - lag * (n_col - 1 - i) < n]
                mine_b = [(i, own_b[t - lag * i]) for i in range(n_col) if 0 <= t - lag * i < n]
                left_sent[t], right_sent[t], tok = hop(
                    tok, z, left_got[t - lag], right_got[t - lag], mine_a, mine_b, t, lag, units, kind[t - lag], kind[t], n_col
                )
            else:
                left_sent[t], right_sent[t] = left_got[t - lag], right_got[t - lag]
                if kind[t - lag][0]:
                    left_sent[t], right_sent[t] = left_sent[t][:, 2 * units:], right_sent[t][:, 2 * units:]
            left_got[t] = lax.ppermute(left_sent[t], ("row", "col"), to_left)
            right_got[t] = lax.ppermute(right_sent[t], ("row", "col"), to_right)
        done = t - lag * (2 * n_col - 2)
        if done >= 0 and done % n_unit == n_unit - 1:
            b = done // n_unit
            hidden = []
            for u in range(n_unit):
                for i, side, at, buf in place(b * n_unit + u):
                    hidden.append((i, side * n_unit + u, at, buf))
            outs[order[b]], tok = project(tok, z, hidden, down, dm, units)

    total = outs[0].astype(jnp.float32)
    for d in order[1:]:
        total = total + lax.ppermute(
            outs[d], "row", [(i, other(i, d)) for i in range(n_row)]
        ).astype(jnp.float32)
    return total.astype(jnp.bfloat16)


def solution(mesh):
    in_specs = (
        P(("groups", "row"), "col"),
        P("col", "row"),
        P("col", "row"),
        P("row", "col"),
        P("col", "row"),
        P("col", "row"),
        P("row", "col"),
    )
    out_specs = P(("groups", "row"), "col")
    body = functools.partial(shards, mesh.shape["row"], mesh.shape["col"])
    return jax.shard_map(body, mesh=mesh, in_specs=in_specs, out_specs=out_specs, check_vma=False)
```

```python
import functools

import jax
import jax.numpy as jnp
from jax import lax
from jax.experimental import pallas as pl
from jax.experimental.pallas import tpu as pltpu
from jax.sharding import PartitionSpec as P

ANY = pl.BlockSpec(memory_space=pl.ANY)
SMEM = pl.BlockSpec(memory_space=pltpu.SMEM)
VMEM = pl.BlockSpec(memory_space=pltpu.VMEM)
MIB = 1 << 20
TOKEN = jax.ShapeDtypeStruct((8, 128), jnp.float32)
BRIEF = pl.CostEstimate(flops=1 << 18, bytes_accessed=1 << 20, transcendentals=0)
LONG = pl.CostEstimate(flops=6 << 30, bytes_accessed=16 << 20, transcendentals=0)


def masked(block, mask, row, col, edge):
    strips = []
    for i in range(block.shape[0] // edge):
        tiles = []
        for j in range(block.shape[1] // edge):
            keep = mask[row + i, col + j].astype(jnp.float32).astype(jnp.bfloat16)
            tiles.append(block[i * edge:(i + 1) * edge, j * edge:(j + 1) * edge] * keep)
        strips.append(jnp.concatenate(tiles, axis=1))
    return jnp.concatenate(strips, axis=0)


def partial_kernel(edge, unit, first, gm_hbm, um_hbm, gate, up, *rest):
    rest, (w, gm, um, sems, mask_sems) = rest[:-5], rest[-5:]
    if first:
        *xs, pa, pb, passed, tok_out = rest
        passed[...] = xs[0][...]
    else:
        tok, *xs, pa, pb, tok_out = rest
    units = w.shape[2]
    starts = (unit * units, gate.shape[1] // 2 + unit * units)
    masks = [pltpu.make_async_copy(gm_hbm, gm, mask_sems.at[0]), pltpu.make_async_copy(um_hbm, um, mask_sems.at[1])]
    plan = [
        (src, mask, start, out, plane)
        for start, out in zip(starts, (pa, pb)) for plane, (src, mask) in enumerate(((gate, gm), (up, um)))
    ]
    loads = [
        pltpu.make_async_copy(src.at[:, pl.ds(start, units)], w.at[i], sems.at[i])
        for i, (src, _, start, _, _) in enumerate(plan)
    ]
    for c in masks + loads:
        c.start()
    for c in masks:
        c.wait()
    x = xs[0][...] if len(xs) == 1 else jnp.concatenate([part[...] for part in xs], axis=0)
    part = min(256, units)
    for i, (_, mask, start, out, plane) in enumerate(plan):
        loads[i].wait()
        for n in range(0, units, part):
            out[plane, :, n:n + part] = jnp.dot(
                x, masked(w[i, :, n:n + part], mask, 0, (start + n) // edge, edge), preferred_element_type=jnp.float32
            ).astype(out.dtype)


def partials(tok, xs, gate, up, gm, um, unit, units):
    rows, depth = xs[0].shape
    out = jax.ShapeDtypeStruct((2, rows * len(xs), units), jnp.bfloat16)
    first = tok is None
    return pl.pallas_call(
        functools.partial(partial_kernel, depth // gm.shape[0], unit, first),
        in_specs=[ANY] * (4 if first else 5) + [VMEM] * len(xs),
        out_specs=[VMEM] * (3 if first else 2) + [ANY],
        out_shape=[out, out] + [jax.ShapeDtypeStruct((rows, depth), jnp.bfloat16)] * first + [TOKEN],
        scratch_shapes=[
            pltpu.VMEM((4, depth, units), jnp.bfloat16),
            pltpu.SMEM(gm.shape, jnp.int32),
            pltpu.SMEM(um.shape, jnp.int32),
            pltpu.SemaphoreType.DMA((4,)),
            pltpu.SemaphoreType.DMA((2,)),
        ],
        input_output_aliases={} if first else {4: 2},
        cost_estimate=LONG,
        compiler_params=pltpu.CompilerParams(vmem_limit_bytes=48 * MIB),
    )(gm, um, gate, up, *([] if first else [tok]), *xs)


def swiglu(gate, up):
    return gate / (1.0 + jnp.exp(-gate)) * up


def over(rows, body):
    piece = min(16, rows)

    def one(i, _):
        body(pl.ds(pl.multiple_of(i * piece, piece), piece))
        return 0

    lax.fori_loop(0, rows // piece, one, 0)


def sum_kernel(own, n_col, goes_on, ends, z_ref, tok, left_in, right_in, *rest):
    n_own = len(own[0]) + len(own[1])
    mine, (*outs, tok_out, a, b, sems) = rest[:n_own], rest[n_own:]
    left_out, right_out = outs[:2] if goes_on else (None, None)
    z = z_ref[0]
    rows = a.shape[1]

    def each(act):
        for ref, (i, row), to, sem in zip(
            mine, own[0] + own[1], [a] * len(own[0]) + [b] * len(own[1]), [0] * len(own[0]) + [1] * len(own[1])
        ):
            @pl.when(z == i)
            def _(ref=ref, row=row, to=to, sem=sem):
                act(pltpu.make_async_copy(ref.at[:, pl.ds(row, rows), :], to, sems.at[sem]))

    each(lambda c: c.start())
    each(lambda c: c.wait())
    for side, came, here, goes, origin, end in (
        (0, left_in, a, left_out, n_col - 1, 0), (1, right_in, b, right_out, 0, n_col - 1)
    ):
        if goes_on:
            @pl.when(z == origin)
            def _(here=here, goes=goes):
                goes[...] = here[...]

            @pl.when((z != origin) & (z != end))
            def _(came=came, here=here, goes=goes):
                def add_up(r):
                    for p in range(2):
                        goes[p, r, :] = (came[p, r, :].astype(jnp.float32) + here[p, r, :].astype(jnp.float32)).astype(goes.dtype)
                over(rows, add_up)
        if ends:
            @pl.when(z == end)
            def _(side=side, came=came, here=here):
                def finish(r):
                    gate, up = (came[p, r, :].astype(jnp.float32) + here[p, r, :].astype(jnp.float32) for p in range(2))
                    outs[-1][side, r, :] = swiglu(gate, up).astype(outs[-1].dtype)
                over(rows, finish)


def sum_step(tok, z, left_in, right_in, own_a, own_b, goes_on, ends, n_col):
    _, rows, units = left_in.shape
    out = jax.ShapeDtypeStruct((2, rows, units), jnp.bfloat16)
    outs = [out] * (2 * goes_on + ends)
    own = (tuple(o[:2] for o in own_a), tuple(o[:2] for o in own_b))
    res = pl.pallas_call(
        functools.partial(sum_kernel, own, n_col, goes_on, ends),
        in_specs=[SMEM, ANY, VMEM, VMEM] + [ANY] * (len(own_a) + len(own_b)),
        out_specs=[VMEM] * len(outs) + [ANY],
        out_shape=outs + [TOKEN],
        scratch_shapes=[
            pltpu.VMEM((2, rows, units), jnp.bfloat16),
            pltpu.VMEM((2, rows, units), jnp.bfloat16),
            pltpu.SemaphoreType.DMA((2,)),
        ],
        input_output_aliases={1: len(outs)},
        cost_estimate=BRIEF,
        compiler_params=pltpu.CompilerParams(vmem_limit_bytes=8 * MIB),
    )(z, tok, left_in, right_in, *[o[2] for o in own_a], *[o[2] for o in own_b])
    sums = res[:2] if goes_on else (None, None)
    return sums, res[-2] if ends else None, res[-1]


def relay_kernel(n_col, made, got, z_ref, tok, *rest):
    fresh, rest = (rest[0], rest[1:]) if made else (None, rest)
    came, (left_out, right_out, tok_out) = rest[:-3], rest[-3:]
    z = z_ref[0]
    for side, out, end in ((0, right_out, 0), (1, left_out, n_col - 1)):
        if made:
            @pl.when(z == end)
            def _(side=side, out=out):
                out[...] = fresh[side]
        if got:
            @pl.when(z != end)
            def _(side=side, out=out):
                out[...] = came[side][...]


def relay(tok, z, fresh, came, n_col):
    like = came[0] if came else fresh
    out = jax.ShapeDtypeStruct(like.shape[-2:], jnp.bfloat16)
    made = fresh is not None
    return pl.pallas_call(
        functools.partial(relay_kernel, n_col, made, len(came) > 0),
        in_specs=[SMEM, ANY] + [VMEM] * (made + len(came)),
        out_specs=[VMEM, VMEM, ANY],
        out_shape=[out, out, TOKEN],
        input_output_aliases={1: 2},
        cost_estimate=LONG,
        compiler_params=pltpu.CompilerParams(vmem_limit_bytes=8 * MIB),
    )(z, tok, *([fresh] if made else []), *came)


def project_kernel(picks, edge, first, n_unit, blocks, more, last, z_ref, mask, tok, down, *rest):
    hidden, rest = rest[:len(picks)], rest[len(picks):]
    if more:
        total, rest = rest[0], rest[1:]
    outs, (tok_out, held, w, sems, w_sems) = rest[:-5], rest[-5:]
    z = z_ref[0]
    units = w.shape[1]
    count = held.shape[0] // 2
    rows = held.shape[1] // blocks
    slabs = 2
    wide = down.shape[1] // slabs

    loads = []
    for j in range(slabs):
        for u in range(count):
            for side in range(2):
                i = (j * count + u) * 2 + side
                row = (side * n_unit + first + u) * units
                part = pl.ds(j * wide, wide)
                loads.append(pltpu.make_async_copy(
                    down.at[pl.ds(row, units), part], w.at[side * count + u, :, part], w_sems.at[i]
                ))
                loads[-1].start()

    def each(act):
        for ref, (i, slot, block) in zip(hidden, picks):
            @pl.when(z == i)
            def _(ref=ref, slot=slot, block=block):
                act(pltpu.make_async_copy(
                    ref, held.at[slot, pl.ds(block * rows, rows), :], sems.at[slot * blocks + block]
                ))

    each(lambda c: c.start())
    each(lambda c: c.wait())
    for j in range(slabs):
        part = slice(j * wide, (j + 1) * wide)
        terms = None
        for u in range(count):
            for side in range(2):
                loads[(j * count + u) * 2 + side].wait()
                slot = side * count + u
                row = (side * n_unit + first + u) * (units // edge)
                term = jnp.dot(
                    held[slot], masked(w[slot, :, part], mask, row, j * (wide // edge), edge),
                    preferred_element_type=jnp.float32,
                )
                terms = term if terms is None else terms + term
        if more:
            terms = terms + total[:, part]
        if last:
            for i, out in enumerate(outs):
                out[:, part] = terms[i * rows:(i + 1) * rows, :].astype(out.dtype)
        else:
            outs[0][:, part] = terms


def project(tok, z, hidden, down, mask, units, first, count, blocks, total, last):
    rows = hidden[0][3].shape[0]
    depth, width = down.shape
    edge = depth // mask.shape[0]
    n_unit = depth // 2 // units
    if last:
        out_shape = [jax.ShapeDtypeStruct((rows, width), jnp.bfloat16)] * blocks
    else:
        out_shape = [jax.ShapeDtypeStruct((blocks * rows, width), jnp.float32)]
    more = total is not None
    aliases = {2: len(out_shape)}
    if more and not last:
        aliases[4 + len(hidden)] = 0
    res = pl.pallas_call(
        functools.partial(project_kernel, tuple(h[:3] for h in hidden), edge, first, n_unit, blocks, more, last),
        in_specs=[SMEM, SMEM, ANY, pl.BlockSpec(memory_space=pltpu.HBM)] + [ANY] * len(hidden) + [VMEM] * more,
        out_specs=[VMEM] * len(out_shape) + [ANY],
        out_shape=out_shape + [TOKEN],
        scratch_shapes=[
            pltpu.VMEM((2 * count, blocks * rows, units), jnp.bfloat16),
            pltpu.VMEM((2 * count, units, width), jnp.bfloat16),
            pltpu.SemaphoreType.DMA((2 * count * blocks,)),
            pltpu.SemaphoreType.DMA((4 * count,)),
        ],
        input_output_aliases=aliases,
        cost_estimate=LONG,
        compiler_params=pltpu.CompilerParams(vmem_limit_bytes=48 * MIB),
    )(z, mask, tok, down, *[h[3] for h in hidden], *([total] if more else []))
    return res[:-1], res[-1]


def add_kernel(tok, x, y, out, tok_out):
    out[...] = (x[...].astype(jnp.float32) + y[...].astype(jnp.float32)).astype(out.dtype)


def add(tok, x, y):
    return pl.pallas_call(
        add_kernel,
        in_specs=[ANY, VMEM, VMEM],
        out_specs=[VMEM, ANY],
        out_shape=[jax.ShapeDtypeStruct(x.shape, x.dtype), TOKEN],
        input_output_aliases={0: 1},
        cost_estimate=BRIEF,
        compiler_params=pltpu.CompilerParams(vmem_limit_bytes=8 * MIB),
    )(tok, x, y)


def cycle(n_row, n_col):
    def at(r, i):
        return r * n_col + (n_col - 1 - i if r % 2 else i)

    steps = []
    for r in range(n_row):
        steps += [(at(r, i), at(r, i + 1)) for i in range(n_col - 1)] + [(at(r, n_col - 1), at(r ^ 1, 0))]
    return steps


def other(i, d, n_row):
    return (i // 2 + d // 2) % (n_row // 2) * 2 + (i % 2 ^ d % 2)


def pieces(group, n_unit):
    count = 2 if n_unit % 2 == 0 else 1
    return [(u, count) for u in range(0, n_unit, count)]


def shards(n_row, n_col, tokens, gate, up, down, gm, um, dm):
    half = gate.shape[1] // 2
    units = min(512, half)
    n_unit = half // units
    rows = tokens.shape[0]
    z, odd = lax.axis_index("col"), lax.axis_index("row") % 2
    z = jnp.where(odd == 1, n_col - 1 - z, z).astype(jnp.int32).reshape(1)
    to_right = cycle(n_row, n_col)
    to_left = [(j, i) for i, j in to_right]
    tok = None

    def swap(x, d, back=False):
        pairs = [(other(i, d, n_row), i) for i in range(n_row)]
        return lax.ppermute(x, "row", [(j, i) for i, j in pairs] if back else pairs)

    groups = [[0]] + [[d, d + 1] for d in range(2, n_row, 2)] + [[1]]
    xs = {0: tokens}
    chunks = [(d, u) for g in groups for u in range(n_unit) for d in g]
    n = len(chunks)
    first_end, last_end = n_col - 1, n + n_col - 2
    last_hop = last_end + n_col - 2
    own_a, own_b = {}, {}
    left_got, right_got, left_on, right_on, left_came, right_came = {}, {}, {}, {}, {}, {}

    def places(k):
        spots = []
        for i in range(n_col):
            t = k + first_end + i
            for side, at, on, came in ((0, i, right_on, right_came), (1, n_col - 1 - i, left_on, left_came)):
                spots.append((at, side, on[t] if t <= last_hop else came[t - 1]))
        return spots

    def compute(group, u):
        def run(tok):
            if tok is None:
                pa, pb, passed, tok = partials(tok, [tokens], gate, up, gm, um, u, units)
                for d in [*range(2, n_row), 1]:
                    xs[d] = swap(passed, d)
            else:
                pa, pb, tok = partials(tok, [xs[d] for d in group], gate, up, gm, um, u, units)
            for i, d in enumerate(group):
                k = chunks.index((d, u))
                own_a[k], own_b[k] = (i * rows, pa), (i * rows, pb)
            return tok
        return run

    totals, outs, pairs = {}, {}, []

    def down_projection(g, first, count):
        def run(tok):
            hidden = []
            for b, d in enumerate(g):
                for u in range(first, first + count):
                    for i, side, buf in places(chunks.index((d, u))):
                        hidden.append((i, side * count + u - first, b, buf))
            key, last = tuple(g), first + count == n_unit
            res, tok = project(tok, z, hidden, down, dm, units, first, count, len(g), totals.get(key), last)
            if last:
                outs.update(zip(g, res))
                if len(g) > 1:
                    pairs.append((g[0], swap(outs.pop(g[1]), 1)))
            else:
                totals[key] = res[0]
            return tok
        return run

    def add_pairs(tok):
        while pairs:
            d, theirs = pairs.pop()
            total, tok = add(tok, outs[d], theirs)
            outs[d] = swap(total, d, back=True)
        return tok

    work = {}
    for g in groups:
        for first, count in pieces(g, n_unit):
            k = max(chunks.index((d, u)) for d in g for u in range(first, first + count))
            work.setdefault(k + 2 * first_end, []).append(down_projection(g, first, count))
    needs = sorted((min(chunks.index((d, u)) for d in g), u, g) for g in groups for u in range(n_unit))
    for k, u, g in reversed(needs):
        at = next((s for s in range(k - 1, -1, -1) if s not in work), k - 1)
        work.setdefault(at, []).insert(0, compute(g, u))

    for run in work.get(-1, []):
        tok = run(tok)
    for t in range(last_hop + 2):
        fresh = None
        if t <= last_end:
            if t == 0:
                sums = own_a[0][1], own_b[0][1]
            else:
                mine_a = [(i, *own_a[t - (n_col - 1 - i)]) for i in range(n_col) if 0 <= t - (n_col - 1 - i) < n]
                mine_b = [(i, *own_b[t - i]) for i in range(n_col) if 0 <= t - i < n]
                sums, fresh, tok = sum_step(
                    tok, z, left_got[t - 1], right_got[t - 1], mine_a, mine_b, t < last_end, t >= first_end, n_col
                )
            if t < last_end:
                left_got[t] = lax.ppermute(sums[0], ("row", "col"), to_left)
                right_got[t] = lax.ppermute(sums[1], ("row", "col"), to_right)
        if first_end <= t <= last_hop:
            came = (right_came[t - 1], left_came[t - 1]) if t > first_end else ()
            left_on[t], right_on[t], tok = relay(tok, z, fresh, came, n_col)
            left_came[t] = lax.ppermute(left_on[t], ("row", "col"), to_left)
            right_came[t] = lax.ppermute(right_on[t], ("row", "col"), to_right)
        tok = add_pairs(tok)
        for run in work.get(t, []):
            tok = run(tok)
    tok = add_pairs(tok)

    mixed = sum(x.astype(jnp.float32) for d, x in outs.items() if d != 1)
    mixed = mixed + swap(outs[1], 1).astype(jnp.float32)
    return mixed.astype(jnp.bfloat16)


def solution(mesh):
    in_specs = (
        P(("groups", "row"), "col"),
        P("col", "row"),
        P("col", "row"),
        P("row", "col"),
        P("col", "row"),
        P("col", "row"),
        P("row", "col"),
    )
    out_specs = P(("groups", "row"), "col")
    body = functools.partial(shards, mesh.shape["row"], mesh.shape["col"])
    return jax.shard_map(body, mesh=mesh, in_specs=in_specs, out_specs=out_specs, check_vma=False)
```

```python
import functools

import jax
import jax.numpy as jnp
from jax import lax
from jax.experimental import pallas as pl
from jax.experimental.pallas import tpu as pltpu
from jax.sharding import PartitionSpec as P

ANY = pl.BlockSpec(memory_space=pl.ANY)
SMEM = pl.BlockSpec(memory_space=pltpu.SMEM)
VMEM = pl.BlockSpec(memory_space=pltpu.VMEM)
MIB = 1 << 20
TOKEN = jax.ShapeDtypeStruct((8, 128), jnp.float32)
BRIEF = pl.CostEstimate(flops=1 << 18, bytes_accessed=1 << 20, transcendentals=0)
LONG = pl.CostEstimate(flops=6 << 30, bytes_accessed=16 << 20, transcendentals=0)


def masked(block, kept, edge):
    strips = []
    for i in range(block.shape[0] // edge):
        tiles = []
        for j in range(block.shape[1] // edge):
            keep = kept(i, j).astype(jnp.float32).astype(jnp.bfloat16)
            tiles.append(block[i * edge:(i + 1) * edge, j * edge:(j + 1) * edge] * keep)
        strips.append(jnp.concatenate(tiles, axis=1))
    return jnp.concatenate(strips, axis=0)


def partial_kernel(edge, unit, first, hand_on, gm_hbm, um_hbm, gate, up, *rest):
    rest, (w, masks, sems, mask_sems) = rest[:-4], rest[-4:]
    *rest, tok_out = rest
    if hand_on:
        *rest, passed = rest
        passed[...] = rest[-3][...]
    *xs, pa, pb = rest if first else rest[1:]
    units = w.shape[2]
    starts = (unit * units, gate.shape[1] // 2 + unit * units)

    def mask_load(plane, src):
        return pltpu.make_async_copy(src, masks.at[plane], mask_sems.at[plane])

    def load(src, side, plane):
        slot = side * 2 + plane
        return pltpu.make_async_copy(src.at[:, pl.ds(starts[side], units)], w.at[slot], sems.at[slot])

    for plane, src in enumerate((gm_hbm, um_hbm)):
        mask_load(plane, src).start()
    for side in range(2):
        for plane, src in enumerate((gate, up)):
            load(src, side, plane).start()
    for plane, src in enumerate((gm_hbm, um_hbm)):
        mask_load(plane, src).wait()
    x = xs[0][...] if len(xs) == 1 else jnp.concatenate([part[...] for part in xs], axis=0)
    part = min(256, units)
    parts = units // part
    for side, out in enumerate((pa, pb)):
        def one(i, _, side=side, out=out):
            plane, n = i // parts, i % parts

            if isinstance(i, int):
                if n == 0:
                    load(gate, side, plane).wait()
                at = pl.ds(n * part, part)
            else:
                @pl.when(n == 0)
                def _():
                    load(gate, side, plane).wait()

                at = pl.ds(pl.multiple_of(n * part, part), part)
            col = starts[side] // edge + n * (part // edge)
            out[plane, :, at] = jnp.dot(
                x, masked(w[side * 2 + plane, :, at], lambda a, b: masks[plane, a, col + b], edge),
                preferred_element_type=jnp.float32,
            ).astype(out.dtype)
            return 0

        if len(xs) > 1:
            for i in range(2 * parts):
                one(i, 0)
        else:
            lax.fori_loop(0, 2 * parts, one, 0)


def partials(tok, xs, gate, up, gm, um, unit, units, hand_on=False):
    rows, depth = xs[0].shape
    out = jax.ShapeDtypeStruct((2, rows * len(xs), units), jnp.bfloat16)
    first = tok is None
    return pl.pallas_call(
        functools.partial(partial_kernel, depth // gm.shape[0], unit, first, hand_on),
        in_specs=[ANY] * (4 if first else 5) + [VMEM] * len(xs),
        out_specs=[VMEM] * (3 if hand_on else 2) + [ANY],
        out_shape=[out, out] + [jax.ShapeDtypeStruct((rows, depth), jnp.bfloat16)] * hand_on + [TOKEN],
        scratch_shapes=[
            pltpu.VMEM((4, depth, units), jnp.bfloat16),
            pltpu.SMEM((2, *gm.shape), jnp.int32),
            pltpu.SemaphoreType.DMA((4,)),
            pltpu.SemaphoreType.DMA((2,)),
        ],
        input_output_aliases={} if first else {4: 3 if hand_on else 2},
        cost_estimate=LONG,
        compiler_params=pltpu.CompilerParams(vmem_limit_bytes=48 * MIB),
    )(gm, um, gate, up, *([] if first else [tok]), *xs)


def swiglu(gate, up):
    return gate / (1.0 + jnp.exp(-gate)) * up


def over(rows, body):
    piece = min(16, rows)

    def one(i, _):
        body(pl.ds(pl.multiple_of(i * piece, piece), piece))
        return 0

    lax.fori_loop(0, rows // piece, one, 0)


def sum_kernel(own, n_col, goes_on, ends, z_ref, tok, left_in, right_in, *rest):
    n_own = len(own[0]) + len(own[1])
    mine, (*outs, tok_out, a, b, sems) = rest[:n_own], rest[n_own:]
    left_out, right_out = outs[:2] if goes_on else (None, None)
    z = z_ref[0]
    rows = a.shape[1]

    def each(act):
        for ref, (i, row), to, sem in zip(
            mine, own[0] + own[1], [a] * len(own[0]) + [b] * len(own[1]), [0] * len(own[0]) + [1] * len(own[1])
        ):
            @pl.when(z == i)
            def _(ref=ref, row=row, to=to, sem=sem):
                act(pltpu.make_async_copy(ref.at[:, pl.ds(row, rows), :], to, sems.at[sem]))

    each(lambda c: c.start())
    each(lambda c: c.wait())
    for side, came, here, goes, origin, end in (
        (0, left_in, a, left_out, n_col - 1, 0), (1, right_in, b, right_out, 0, n_col - 1)
    ):
        if goes_on:
            @pl.when(z == origin)
            def _(here=here, goes=goes):
                goes[...] = here[...]

            @pl.when((z != origin) & (z != end))
            def _(came=came, here=here, goes=goes):
                def add_up(r):
                    for p in range(2):
                        goes[p, r, :] = (came[p, r, :].astype(jnp.float32) + here[p, r, :].astype(jnp.float32)).astype(goes.dtype)
                over(rows, add_up)
        if ends:
            @pl.when(z == end)
            def _(side=side, came=came, here=here):
                def finish(r):
                    gate, up = (came[p, r, :].astype(jnp.float32) + here[p, r, :].astype(jnp.float32) for p in range(2))
                    outs[-1][side, r, :] = swiglu(gate, up).astype(outs[-1].dtype)
                over(rows, finish)


def sum_step(tok, z, left_in, right_in, own_a, own_b, goes_on, ends, n_col):
    _, rows, units = left_in.shape
    out = jax.ShapeDtypeStruct((2, rows, units), jnp.bfloat16)
    outs = [out] * (2 * goes_on + ends)
    own = (tuple(o[:2] for o in own_a), tuple(o[:2] for o in own_b))
    res = pl.pallas_call(
        functools.partial(sum_kernel, own, n_col, goes_on, ends),
        in_specs=[SMEM, ANY, VMEM, VMEM] + [ANY] * (len(own_a) + len(own_b)),
        out_specs=[VMEM] * len(outs) + [ANY],
        out_shape=outs + [TOKEN],
        scratch_shapes=[
            pltpu.VMEM((2, rows, units), jnp.bfloat16),
            pltpu.VMEM((2, rows, units), jnp.bfloat16),
            pltpu.SemaphoreType.DMA((2,)),
        ],
        input_output_aliases={1: len(outs)},
        cost_estimate=BRIEF,
        compiler_params=pltpu.CompilerParams(vmem_limit_bytes=8 * MIB),
    )(z, tok, left_in, right_in, *[o[2] for o in own_a], *[o[2] for o in own_b])
    sums = res[:2] if goes_on else (None, None)
    return sums, res[-2] if ends else None, res[-1]


def relay_kernel(n_col, made, got, z_ref, tok, *rest):
    fresh, rest = (rest[0], rest[1:]) if made else (None, rest)
    came, (left_out, right_out, tok_out) = rest[:-3], rest[-3:]
    z = z_ref[0]
    for side, out, end in ((0, right_out, 0), (1, left_out, n_col - 1)):
        if made:
            @pl.when(z == end)
            def _(side=side, out=out):
                out[...] = fresh[side]
        if got:
            @pl.when(z != end)
            def _(side=side, out=out):
                out[...] = came[side][...]


def relay(tok, z, fresh, came, n_col):
    like = came[0] if came else fresh
    out = jax.ShapeDtypeStruct(like.shape[-2:], jnp.bfloat16)
    made = fresh is not None
    return pl.pallas_call(
        functools.partial(relay_kernel, n_col, made, len(came) > 0),
        in_specs=[SMEM, ANY] + [VMEM] * (made + len(came)),
        out_specs=[VMEM, VMEM, ANY],
        out_shape=[out, out, TOKEN],
        input_output_aliases={1: 2},
        cost_estimate=LONG,
        compiler_params=pltpu.CompilerParams(vmem_limit_bytes=8 * MIB),
    )(z, tok, *([fresh] if made else []), *came)


def project_kernel(picks, edge, first, n_unit, blocks, more, last, unroll, z_ref, mask, tok, down, *rest):
    hidden, rest = rest[:len(picks)], rest[len(picks):]
    if more:
        total, rest = rest[0], rest[1:]
    outs, (tok_out, held, w, sems, w_sems) = rest[:-5], rest[-5:]
    z = z_ref[0]
    units = w.shape[1]
    count = held.shape[0] // 2
    rows = held.shape[1] // blocks
    slabs = 2
    wide = down.shape[1] // slabs
    thin = wide // 2

    def load(j, u, side):
        row = (side * n_unit + first + u) * units
        at = pl.ds(j * wide, wide)
        slot = side * count + u
        return pltpu.make_async_copy(
            down.at[pl.ds(row, units), at], w.at[slot, :, at], w_sems.at[j * (2 * count) + slot]
        )

    def every(act, j):
        for u in range(count):
            for side in range(2):
                act(load(j, u, side))

    for j in range(slabs):
        every(lambda c: c.start(), j)

    def each(act):
        for ref, (i, slot, block) in zip(hidden, picks):
            @pl.when(z == i)
            def _(ref=ref, slot=slot, block=block):
                act(pltpu.make_async_copy(
                    ref, held.at[slot, pl.ds(block * rows, rows), :], sems.at[slot * blocks + block]
                ))

    each(lambda c: c.start())
    each(lambda c: c.wait())

    def one(i, _):
        if unroll:
            if i % 2 == 0:
                every(lambda c: c.wait(), i // 2)
            at = pl.ds(i * thin, thin)
        else:
            for j in range(slabs):
                @pl.when(i == 2 * j)
                def _(j=j):
                    every(lambda c: c.wait(), j)

            at = pl.ds(pl.multiple_of(i * thin, thin), thin)
        terms = None
        for u in range(count):
            for side in range(2):
                slot = side * count + u
                row = (side * n_unit + first + u) * (units // edge)
                kept = masked(w[slot, :, at], lambda a, b: mask[row + a, i * (thin // edge) + b], edge)
                term = jnp.dot(held[slot], kept, preferred_element_type=jnp.float32)
                terms = term if terms is None else terms + term
        if more:
            terms = terms + total[:, at]
        if last:
            for k, out in enumerate(outs):
                out[:, at] = terms[k * rows:(k + 1) * rows, :].astype(out.dtype)
        else:
            outs[0][:, at] = terms
        return 0

    if unroll:
        for i in range(2 * slabs):
            one(i, 0)
    else:
        lax.fori_loop(0, 2 * slabs, one, 0)


def project(tok, z, hidden, down, mask, units, first, count, blocks, total, last, unroll):
    rows = hidden[0][3].shape[0]
    depth, width = down.shape
    edge = depth // mask.shape[0]
    n_unit = depth // 2 // units
    if last:
        out_shape = [jax.ShapeDtypeStruct((rows, width), jnp.bfloat16)] * blocks
    else:
        out_shape = [jax.ShapeDtypeStruct((blocks * rows, width), jnp.float32)]
    more = total is not None
    aliases = {2: len(out_shape)}
    if more and not last:
        aliases[4 + len(hidden)] = 0
    res = pl.pallas_call(
        functools.partial(project_kernel, tuple(h[:3] for h in hidden), edge, first, n_unit, blocks, more, last, unroll),
        in_specs=[SMEM, SMEM, ANY, pl.BlockSpec(memory_space=pltpu.HBM)] + [ANY] * len(hidden) + [VMEM] * more,
        out_specs=[VMEM] * len(out_shape) + [ANY],
        out_shape=out_shape + [TOKEN],
        scratch_shapes=[
            pltpu.VMEM((2 * count, blocks * rows, units), jnp.bfloat16),
            pltpu.VMEM((2 * count, units, width), jnp.bfloat16),
            pltpu.SemaphoreType.DMA((2 * count * blocks,)),
            pltpu.SemaphoreType.DMA((4 * count,)),
        ],
        input_output_aliases=aliases,
        cost_estimate=LONG,
        compiler_params=pltpu.CompilerParams(vmem_limit_bytes=48 * MIB),
    )(z, mask, tok, down, *[h[3] for h in hidden], *([total] if more else []))
    return res[:-1], res[-1]


def add_kernel(tok, x, y, out, tok_out):
    out[...] = (x[...].astype(jnp.float32) + y[...].astype(jnp.float32)).astype(out.dtype)


def add(tok, x, y):
    return pl.pallas_call(
        add_kernel,
        in_specs=[ANY, VMEM, VMEM],
        out_specs=[VMEM, ANY],
        out_shape=[jax.ShapeDtypeStruct(x.shape, x.dtype), TOKEN],
        input_output_aliases={0: 1},
        cost_estimate=BRIEF,
        compiler_params=pltpu.CompilerParams(vmem_limit_bytes=8 * MIB),
    )(tok, x, y)


def cycle(n_row, n_col):
    def at(r, i):
        return r * n_col + (n_col - 1 - i if r % 2 else i)

    steps = []
    for r in range(n_row):
        steps += [(at(r, i), at(r, i + 1)) for i in range(n_col - 1)] + [(at(r, n_col - 1), at(r ^ 1, 0))]
    return steps


def other(i, d, n_row):
    return (i // 2 + d // 2) % (n_row // 2) * 2 + (i % 2 ^ d % 2)


def pieces(group, n_unit):
    count = 2 if n_unit % 2 == 0 else 1
    return [(u, count) for u in range(0, n_unit, count)]


def shards(n_row, n_col, tokens, gate, up, down, gm, um, dm):
    half = gate.shape[1] // 2
    units = min(512, half)
    n_unit = half // units
    rows = tokens.shape[0]
    z, odd = lax.axis_index("col"), lax.axis_index("row") % 2
    z = jnp.where(odd == 1, n_col - 1 - z, z).astype(jnp.int32).reshape(1)
    to_right = cycle(n_row, n_col)
    to_left = [(j, i) for i, j in to_right]
    tok = None

    def swap(x, d, back=False):
        pairs = [(other(i, d, n_row), i) for i in range(n_row)]
        return lax.ppermute(x, "row", [(j, i) for i, j in pairs] if back else pairs)

    groups = [[0]] + [[d, d + 1] for d in range(2, n_row, 2)] + [[1]]
    xs = {0: tokens}
    chunks = [(d, u) for g in groups for u in range(n_unit) for d in g]
    n = len(chunks)
    first_end, last_end = n_col - 1, n + n_col - 2
    last_hop = last_end + n_col - 2
    own_a, own_b = {}, {}
    left_got, right_got, left_on, right_on, left_came, right_came = {}, {}, {}, {}, {}, {}

    def places(k):
        spots = []
        for i in range(n_col):
            t = k + first_end + i
            for side, at, on, came in ((0, i, right_on, right_came), (1, n_col - 1 - i, left_on, left_came)):
                spots.append((at, side, on[t] if t <= last_hop else came[t - 1]))
        return spots

    def compute(group, u):
        def run(tok):
            hand_on = group == [0] and u == min(1, n_unit - 1)
            pa, pb, *passed, tok = partials(tok, [xs[d] for d in group], gate, up, gm, um, u, units, hand_on)
            if hand_on:
                for d in [*range(2, n_row), 1]:
                    xs[d] = swap(passed[0], d)
            for i, d in enumerate(group):
                k = chunks.index((d, u))
                own_a[k], own_b[k] = (i * rows, pa), (i * rows, pb)
            return tok
        return run

    totals, outs, pairs = {}, {}, []

    def down_projection(g, first, count):
        def run(tok):
            hidden = []
            for b, d in enumerate(g):
                for u in range(first, first + count):
                    for i, side, buf in places(chunks.index((d, u))):
                        hidden.append((i, side * count + u - first, b, buf))
            key, last = tuple(g), first + count == n_unit
            res, tok = project(tok, z, hidden, down, dm, units, first, count, len(g), totals.get(key), last, g == [1])
            if last:
                outs.update(zip(g, res))
                if len(g) > 1:
                    pairs.append((g[0], swap(outs.pop(g[1]), 1)))
            else:
                totals[key] = res[0]
            return tok
        return run

    def add_pairs(tok):
        while pairs:
            d, theirs = pairs.pop()
            total, tok = add(tok, outs[d], theirs)
            outs[d] = swap(total, d, back=True)
        return tok

    work = {}
    for g in groups:
        for first, count in pieces(g, n_unit):
            k = max(chunks.index((d, u)) for d in g for u in range(first, first + count))
            work.setdefault(k + 2 * first_end, []).append(down_projection(g, first, count))
    needs = sorted((min(chunks.index((d, u)) for d in g), u, g) for g in groups for u in range(n_unit))
    for k, u, g in reversed(needs):
        at = next((s for s in range(k - 1, -1, -1) if s not in work), k - 1)
        work.setdefault(at, []).insert(0, compute(g, u))

    for run in work.get(-1, []):
        tok = run(tok)
    for t in range(last_hop + 2):
        fresh = None
        if t <= last_end:
            if t == 0:
                sums = own_a[0][1], own_b[0][1]
            else:
                mine_a = [(i, *own_a[t - (n_col - 1 - i)]) for i in range(n_col) if 0 <= t - (n_col - 1 - i) < n]
                mine_b = [(i, *own_b[t - i]) for i in range(n_col) if 0 <= t - i < n]
                sums, fresh, tok = sum_step(
                    tok, z, left_got[t - 1], right_got[t - 1], mine_a, mine_b, t < last_end, t >= first_end, n_col
                )
            if t < last_end:
                left_got[t] = lax.ppermute(sums[0], ("row", "col"), to_left)
                right_got[t] = lax.ppermute(sums[1], ("row", "col"), to_right)
        if first_end <= t <= last_hop:
            came = (right_came[t - 1], left_came[t - 1]) if t > first_end else ()
            left_on[t], right_on[t], tok = relay(tok, z, fresh, came, n_col)
            left_came[t] = lax.ppermute(left_on[t], ("row", "col"), to_left)
            right_came[t] = lax.ppermute(right_on[t], ("row", "col"), to_right)
        tok = add_pairs(tok)
        for run in work.get(t, []):
            tok = run(tok)
    tok = add_pairs(tok)

    mixed = sum(x.astype(jnp.float32) for d, x in outs.items() if d != 1)
    mixed = mixed + swap(outs[1], 1).astype(jnp.float32)
    return mixed.astype(jnp.bfloat16)


def solution(mesh):
    in_specs = (
        P(("groups", "row"), "col"),
        P("col", "row"),
        P("col", "row"),
        P("row", "col"),
        P("col", "row"),
        P("col", "row"),
        P("row", "col"),
    )
    out_specs = P(("groups", "row"), "col")
    body = functools.partial(shards, mesh.shape["row"], mesh.shape["col"])
    return jax.shard_map(body, mesh=mesh, in_specs=in_specs, out_specs=out_specs, check_vma=False)
```

```python
import functools

import jax
import jax.numpy as jnp
from jax import lax
from jax.experimental import pallas as pl
from jax.experimental.pallas import tpu as pltpu
from jax.sharding import PartitionSpec as P

ANY = pl.BlockSpec(memory_space=pl.ANY)
SMEM = pl.BlockSpec(memory_space=pltpu.SMEM)
VMEM = pl.BlockSpec(memory_space=pltpu.VMEM)
MIB = 1 << 20
TOKEN = jax.ShapeDtypeStruct((8, 128), jnp.float32)
BRIEF = pl.CostEstimate(flops=1 << 18, bytes_accessed=1 << 20, transcendentals=0)
LONG = pl.CostEstimate(flops=6 << 30, bytes_accessed=16 << 20, transcendentals=0)


def masked(block, kept, edge):
    strips = []
    for i in range(block.shape[0] // edge):
        tiles = []
        for j in range(block.shape[1] // edge):
            keep = kept(i, j).astype(jnp.float32).astype(jnp.bfloat16)
            tiles.append(block[i * edge:(i + 1) * edge, j * edge:(j + 1) * edge] * keep)
        strips.append(jnp.concatenate(tiles, axis=1))
    return jnp.concatenate(strips, axis=0)


def partial_kernel(edge, unit, first, hand_on, unroll, gm_hbm, um_hbm, gate, up, *rest):
    rest, (w, masks, sems, mask_sems) = rest[:-4], rest[-4:]
    *rest, tok_out = rest
    if hand_on:
        *rest, passed = rest
        passed[...] = rest[-3][...]
    *xs, pa, pb = rest if first else rest[1:]
    units = w.shape[2]
    starts = (unit * units, gate.shape[1] // 2 + unit * units)

    def mask_load(plane, src):
        return pltpu.make_async_copy(src, masks.at[plane], mask_sems.at[plane])

    def load(src, side, plane):
        slot = side * 2 + plane
        return pltpu.make_async_copy(src.at[:, pl.ds(starts[side], units)], w.at[slot], sems.at[slot])

    for plane, src in enumerate((gm_hbm, um_hbm)):
        mask_load(plane, src).start()
    for side in range(2):
        for plane, src in enumerate((gate, up)):
            load(src, side, plane).start()
    for plane, src in enumerate((gm_hbm, um_hbm)):
        mask_load(plane, src).wait()
    x = xs[0][...] if len(xs) == 1 else jnp.concatenate([part[...] for part in xs], axis=0)
    part = min(256, units)
    parts = units // part
    for side, out in enumerate((pa, pb)):
        def one(i, _, side=side, out=out):
            plane, n = i // parts, i % parts

            if isinstance(i, int):
                if n == 0:
                    load(gate, side, plane).wait()
                at = pl.ds(n * part, part)
            else:
                @pl.when(n == 0)
                def _():
                    load(gate, side, plane).wait()

                at = pl.ds(pl.multiple_of(n * part, part), part)
            col = starts[side] // edge + n * (part // edge)
            out[plane, :, at] = jnp.dot(
                x, masked(w[side * 2 + plane, :, at], lambda a, b: masks[plane, a, col + b], edge),
                preferred_element_type=jnp.float32,
            ).astype(out.dtype)
            return 0

        if unroll:
            for i in range(2 * parts):
                one(i, 0)
        else:
            lax.fori_loop(0, 2 * parts, one, 0)


def partials(tok, xs, gate, up, gm, um, unit, units, hand_on, unroll):
    rows, depth = xs[0].shape
    out = jax.ShapeDtypeStruct((2, rows * len(xs), units), jnp.bfloat16)
    first = tok is None
    return pl.pallas_call(
        functools.partial(partial_kernel, depth // gm.shape[0], unit, first, hand_on, unroll),
        in_specs=[ANY] * (4 if first else 5) + [VMEM] * len(xs),
        out_specs=[VMEM] * (3 if hand_on else 2) + [ANY],
        out_shape=[out, out] + [jax.ShapeDtypeStruct((rows, depth), jnp.bfloat16)] * hand_on + [TOKEN],
        scratch_shapes=[
            pltpu.VMEM((4, depth, units), jnp.bfloat16),
            pltpu.SMEM((2, *gm.shape), jnp.int32),
            pltpu.SemaphoreType.DMA((4,)),
            pltpu.SemaphoreType.DMA((2,)),
        ],
        input_output_aliases={} if first else {4: 3 if hand_on else 2},
        cost_estimate=LONG,
        compiler_params=pltpu.CompilerParams(vmem_limit_bytes=(46 if unroll else 48) * MIB),
    )(gm, um, gate, up, *([] if first else [tok]), *xs)


def swiglu(gate, up):
    return gate / (1.0 + jnp.exp(-gate)) * up


def over(rows, body):
    piece = min(16, rows)

    def one(i, _):
        body(pl.ds(pl.multiple_of(i * piece, piece), piece))
        return 0

    lax.fori_loop(0, rows // piece, one, 0)


def sum_kernel(own, n_col, goes_on, ends, z_ref, tok, left_in, right_in, *rest):
    n_own = len(own[0]) + len(own[1])
    mine, (*outs, tok_out, a, b, sems) = rest[:n_own], rest[n_own:]
    left_out, right_out = outs[:2] if goes_on else (None, None)
    z = z_ref[0]
    rows = a.shape[1]

    def each(act):
        for ref, (i, row), to, sem in zip(
            mine, own[0] + own[1], [a] * len(own[0]) + [b] * len(own[1]), [0] * len(own[0]) + [1] * len(own[1])
        ):
            @pl.when(z == i)
            def _(ref=ref, row=row, to=to, sem=sem):
                act(pltpu.make_async_copy(ref.at[:, pl.ds(row, rows), :], to, sems.at[sem]))

    each(lambda c: c.start())
    each(lambda c: c.wait())
    for side, came, here, goes, origin, end in (
        (0, left_in, a, left_out, n_col - 1, 0), (1, right_in, b, right_out, 0, n_col - 1)
    ):
        if goes_on:
            @pl.when(z == origin)
            def _(here=here, goes=goes):
                goes[...] = here[...]

            @pl.when((z != origin) & (z != end))
            def _(came=came, here=here, goes=goes):
                def add_up(r):
                    for p in range(2):
                        goes[p, r, :] = (came[p, r, :].astype(jnp.float32) + here[p, r, :].astype(jnp.float32)).astype(goes.dtype)
                over(rows, add_up)
        if ends:
            @pl.when(z == end)
            def _(side=side, came=came, here=here):
                def finish(r):
                    gate, up = (came[p, r, :].astype(jnp.float32) + here[p, r, :].astype(jnp.float32) for p in range(2))
                    outs[-1][side, r, :] = swiglu(gate, up).astype(outs[-1].dtype)
                over(rows, finish)


def sum_step(tok, z, left_in, right_in, own_a, own_b, goes_on, ends, n_col):
    _, rows, units = left_in.shape
    out = jax.ShapeDtypeStruct((2, rows, units), jnp.bfloat16)
    outs = [out] * (2 * goes_on + ends)
    own = (tuple(o[:2] for o in own_a), tuple(o[:2] for o in own_b))
    res = pl.pallas_call(
        functools.partial(sum_kernel, own, n_col, goes_on, ends),
        in_specs=[SMEM, ANY, VMEM, VMEM] + [ANY] * (len(own_a) + len(own_b)),
        out_specs=[VMEM] * len(outs) + [ANY],
        out_shape=outs + [TOKEN],
        scratch_shapes=[
            pltpu.VMEM((2, rows, units), jnp.bfloat16),
            pltpu.VMEM((2, rows, units), jnp.bfloat16),
            pltpu.SemaphoreType.DMA((2,)),
        ],
        input_output_aliases={1: len(outs)},
        cost_estimate=BRIEF,
        compiler_params=pltpu.CompilerParams(vmem_limit_bytes=8 * MIB),
    )(z, tok, left_in, right_in, *[o[2] for o in own_a], *[o[2] for o in own_b])
    sums = res[:2] if goes_on else (None, None)
    return sums, res[-2] if ends else None, res[-1]


def relay_kernel(n_col, made, got, z_ref, tok, *rest):
    fresh, rest = (rest[0], rest[1:]) if made else (None, rest)
    came, (left_out, right_out, tok_out) = rest[:-3], rest[-3:]
    z = z_ref[0]
    for side, out, end in ((0, right_out, 0), (1, left_out, n_col - 1)):
        if made:
            @pl.when(z == end)
            def _(side=side, out=out):
                out[...] = fresh[side]
        if got:
            @pl.when(z != end)
            def _(side=side, out=out):
                out[...] = came[side][...]


def relay(tok, z, fresh, came, n_col):
    like = came[0] if came else fresh
    out = jax.ShapeDtypeStruct(like.shape[-2:], jnp.bfloat16)
    made = fresh is not None
    return pl.pallas_call(
        functools.partial(relay_kernel, n_col, made, len(came) > 0),
        in_specs=[SMEM, ANY] + [VMEM] * (made + len(came)),
        out_specs=[VMEM, VMEM, ANY],
        out_shape=[out, out, TOKEN],
        input_output_aliases={1: 2},
        cost_estimate=LONG,
        compiler_params=pltpu.CompilerParams(vmem_limit_bytes=8 * MIB),
    )(z, tok, *([fresh] if made else []), *came)


def project_kernel(picks, edge, first, n_unit, blocks, more, last, unroll, z_ref, mask, tok, down, *rest):
    hidden, rest = rest[:len(picks)], rest[len(picks):]
    if more:
        total, rest = rest[0], rest[1:]
    outs, (tok_out, held, w, sems, w_sems) = rest[:-5], rest[-5:]
    z = z_ref[0]
    units = w.shape[1]
    count = held.shape[0] // 2
    rows = held.shape[1] // blocks
    slabs = 2
    wide = down.shape[1] // slabs
    thin = wide // 2

    def load(j, u, side):
        row = (side * n_unit + first + u) * units
        at = pl.ds(j * wide, wide)
        slot = side * count + u
        return pltpu.make_async_copy(
            down.at[pl.ds(row, units), at], w.at[slot, :, at], w_sems.at[j * (2 * count) + slot]
        )

    def every(act, j):
        for u in range(count):
            for side in range(2):
                act(load(j, u, side))

    for j in range(slabs):
        every(lambda c: c.start(), j)

    def each(act):
        for ref, (i, slot, block) in zip(hidden, picks):
            @pl.when(z == i)
            def _(ref=ref, slot=slot, block=block):
                act(pltpu.make_async_copy(
                    ref, held.at[slot, pl.ds(block * rows, rows), :], sems.at[slot * blocks + block]
                ))

    each(lambda c: c.start())
    each(lambda c: c.wait())

    def one(i, _):
        if unroll:
            if i % 2 == 0:
                every(lambda c: c.wait(), i // 2)
            at = pl.ds(i * thin, thin)
        else:
            for j in range(slabs):
                @pl.when(i == 2 * j)
                def _(j=j):
                    every(lambda c: c.wait(), j)

            at = pl.ds(pl.multiple_of(i * thin, thin), thin)
        terms = None
        for u in range(count):
            for side in range(2):
                slot = side * count + u
                row = (side * n_unit + first + u) * (units // edge)
                kept = masked(w[slot, :, at], lambda a, b: mask[row + a, i * (thin // edge) + b], edge)
                term = jnp.dot(held[slot], kept, preferred_element_type=jnp.float32)
                terms = term if terms is None else terms + term
        if more:
            terms = terms + total[:, at]
        if last:
            for k, out in enumerate(outs):
                out[:, at] = terms[k * rows:(k + 1) * rows, :].astype(out.dtype)
        else:
            outs[0][:, at] = terms
        return 0

    if unroll:
        for i in range(2 * slabs):
            one(i, 0)
    else:
        lax.fori_loop(0, 2 * slabs, one, 0)


def project(tok, z, hidden, down, mask, units, first, count, blocks, total, last, unroll):
    rows = hidden[0][3].shape[0]
    depth, width = down.shape
    edge = depth // mask.shape[0]
    n_unit = depth // 2 // units
    if last:
        out_shape = [jax.ShapeDtypeStruct((rows, width), jnp.bfloat16)] * blocks
    else:
        out_shape = [jax.ShapeDtypeStruct((blocks * rows, width), jnp.float32)]
    more = total is not None
    aliases = {2: len(out_shape)}
    if more and not last:
        aliases[4 + len(hidden)] = 0
    res = pl.pallas_call(
        functools.partial(project_kernel, tuple(h[:3] for h in hidden), edge, first, n_unit, blocks, more, last, unroll),
        in_specs=[SMEM, SMEM, ANY, pl.BlockSpec(memory_space=pltpu.HBM)] + [ANY] * len(hidden) + [VMEM] * more,
        out_specs=[VMEM] * len(out_shape) + [ANY],
        out_shape=out_shape + [TOKEN],
        scratch_shapes=[
            pltpu.VMEM((2 * count, blocks * rows, units), jnp.bfloat16),
            pltpu.VMEM((2 * count, units, width), jnp.bfloat16),
            pltpu.SemaphoreType.DMA((2 * count * blocks,)),
            pltpu.SemaphoreType.DMA((4 * count,)),
        ],
        input_output_aliases=aliases,
        cost_estimate=LONG,
        compiler_params=pltpu.CompilerParams(vmem_limit_bytes=46 * MIB),
    )(z, mask, tok, down, *[h[3] for h in hidden], *([total] if more else []))
    return res[:-1], res[-1]


def add_kernel(tok, x, y, out, tok_out):
    out[...] = (x[...].astype(jnp.float32) + y[...].astype(jnp.float32)).astype(out.dtype)


def add(tok, x, y):
    return pl.pallas_call(
        add_kernel,
        in_specs=[ANY, VMEM, VMEM],
        out_specs=[VMEM, ANY],
        out_shape=[jax.ShapeDtypeStruct(x.shape, x.dtype), TOKEN],
        input_output_aliases={0: 1},
        cost_estimate=BRIEF,
        compiler_params=pltpu.CompilerParams(vmem_limit_bytes=8 * MIB),
    )(tok, x, y)


def cycle(n_row, n_col):
    def at(r, i):
        return r * n_col + (n_col - 1 - i if r % 2 else i)

    steps = []
    for r in range(n_row):
        steps += [(at(r, i), at(r, i + 1)) for i in range(n_col - 1)] + [(at(r, n_col - 1), at(r ^ 1, 0))]
    return steps


def other(i, d, n_row):
    return (i // 2 + d // 2) % (n_row // 2) * 2 + (i % 2 ^ d % 2)


def pieces(group, n_unit):
    if n_unit % 2 or group == [1]:
        return [(u, 1) for u in range(n_unit)]
    halves = [(u, 2) for u in range(0, n_unit, 2)]
    return halves if group == [0] else halves[:-1] + [(n_unit - 2, 1), (n_unit - 1, 1)]


def shards(n_row, n_col, tokens, gate, up, down, gm, um, dm):
    half = gate.shape[1] // 2
    units = min(512, half)
    n_unit = half // units
    rows = tokens.shape[0]
    z, odd = lax.axis_index("col"), lax.axis_index("row") % 2
    z = jnp.where(odd == 1, n_col - 1 - z, z).astype(jnp.int32).reshape(1)
    to_right = cycle(n_row, n_col)
    to_left = [(j, i) for i, j in to_right]
    tok = None

    def swap(x, d, back=False):
        pairs = [(other(i, d, n_row), i) for i in range(n_row)]
        return lax.ppermute(x, "row", [(j, i) for i, j in pairs] if back else pairs)

    groups = [[0]] + [[d, d + 1] for d in range(2, n_row, 2)] + [[1]]
    xs = {0: tokens}
    chunks = [(d, u) for g in groups for u in range(n_unit) for d in g]
    n = len(chunks)
    first_end, last_end = n_col - 1, n + n_col - 2
    last_hop = last_end + n_col - 2
    own_a, own_b = {}, {}
    left_got, right_got, left_on, right_on, left_came, right_came = {}, {}, {}, {}, {}, {}

    def places(k):
        spots = []
        for i in range(n_col):
            t = k + first_end + i
            for side, at, on, came in ((0, i, right_on, right_came), (1, n_col - 1 - i, left_on, left_came)):
                spots.append((at, side, on[t] if t <= last_hop else came[t - 1]))
        return spots

    def compute(group, u):
        def run(tok):
            hand_on = group == [0] and u == min(1, n_unit - 1)
            pa, pb, *passed, tok = partials(tok, [xs[d] for d in group], gate, up, gm, um, u, units, hand_on, group != [0])
            if hand_on:
                for d in [*range(2, n_row), 1]:
                    xs[d] = swap(passed[0], d)
            for i, d in enumerate(group):
                k = chunks.index((d, u))
                own_a[k], own_b[k] = (i * rows, pa), (i * rows, pb)
            return tok
        return run

    totals, outs, pairs = {}, {}, []

    def down_projection(g, first, count):
        def run(tok):
            hidden = []
            for b, d in enumerate(g):
                for u in range(first, first + count):
                    for i, side, buf in places(chunks.index((d, u))):
                        hidden.append((i, side * count + u - first, b, buf))
            key, last = tuple(g), first + count == n_unit
            res, tok = project(tok, z, hidden, down, dm, units, first, count, len(g), totals.get(key), last, g == [1] and last)
            if last:
                outs.update(zip(g, res))
                if len(g) > 1:
                    pairs.append((g[0], swap(outs.pop(g[1]), 1)))
            else:
                totals[key] = res[0]
            return tok
        return run

    def add_pairs(tok):
        while pairs:
            d, theirs = pairs.pop()
            total, tok = add(tok, outs[d], theirs)
            outs[d] = swap(total, d, back=True)
        return tok

    work = {}
    for g in groups:
        for first, count in pieces(g, n_unit):
            k = max(chunks.index((d, u)) for d in g for u in range(first, first + count))
            work.setdefault(k + 2 * first_end, []).append(down_projection(g, first, count))
    needs = sorted((min(chunks.index((d, u)) for d in g), u, g) for g in groups for u in range(n_unit))
    for k, u, g in reversed(needs):
        at = next((s for s in range(k - 1, -1, -1) if s not in work), k - 1)
        work.setdefault(at, []).insert(0, compute(g, u))

    for run in work.get(-1, []):
        tok = run(tok)
    for t in range(last_hop + 2):
        fresh = None
        if t <= last_end:
            if t == 0:
                sums = own_a[0][1], own_b[0][1]
            else:
                mine_a = [(i, *own_a[t - (n_col - 1 - i)]) for i in range(n_col) if 0 <= t - (n_col - 1 - i) < n]
                mine_b = [(i, *own_b[t - i]) for i in range(n_col) if 0 <= t - i < n]
                sums, fresh, tok = sum_step(
                    tok, z, left_got[t - 1], right_got[t - 1], mine_a, mine_b, t < last_end, t >= first_end, n_col
                )
            if t < last_end:
                left_got[t] = lax.ppermute(sums[0], ("row", "col"), to_left)
                right_got[t] = lax.ppermute(sums[1], ("row", "col"), to_right)
        if first_end <= t <= last_hop:
            came = (right_came[t - 1], left_came[t - 1]) if t > first_end else ()
            left_on[t], right_on[t], tok = relay(tok, z, fresh, came, n_col)
            left_came[t] = lax.ppermute(left_on[t], ("row", "col"), to_left)
            right_came[t] = lax.ppermute(right_on[t], ("row", "col"), to_right)
        tok = add_pairs(tok)
        for run in work.get(t, []):
            tok = run(tok)
    tok = add_pairs(tok)

    mixed = sum(x.astype(jnp.float32) for d, x in outs.items() if d != 1)
    mixed = mixed + swap(outs[1], 1).astype(jnp.float32)
    return mixed.astype(jnp.bfloat16)


def solution(mesh):
    in_specs = (
        P(("groups", "row"), "col"),
        P("col", "row"),
        P("col", "row"),
        P("row", "col"),
        P("col", "row"),
        P("col", "row"),
        P("row", "col"),
    )
    out_specs = P(("groups", "row"), "col")
    body = functools.partial(shards, mesh.shape["row"], mesh.shape["col"])
    return jax.shard_map(body, mesh=mesh, in_specs=in_specs, out_specs=out_specs, check_vma=False)
```

```python
import functools

import jax
import jax.numpy as jnp
from jax import lax
from jax.experimental import pallas as pl
from jax.experimental.pallas import tpu as pltpu
from jax.sharding import PartitionSpec as P

ANY = pl.BlockSpec(memory_space=pl.ANY)
SMEM = pl.BlockSpec(memory_space=pltpu.SMEM)
VMEM = pl.BlockSpec(memory_space=pltpu.VMEM)
MIB = 1 << 20
TOKEN = jax.ShapeDtypeStruct((8, 128), jnp.float32)
BRIEF = pl.CostEstimate(flops=1 << 18, bytes_accessed=1 << 20, transcendentals=0)
LONG = pl.CostEstimate(flops=6 << 30, bytes_accessed=16 << 20, transcendentals=0)


def masked(block, kept, edge):
    strips = []
    for i in range(block.shape[0] // edge):
        tiles = []
        for j in range(block.shape[1] // edge):
            keep = kept(i, j).astype(jnp.float32).astype(jnp.bfloat16)
            tiles.append(block[i * edge:(i + 1) * edge, j * edge:(j + 1) * edge] * keep)
        strips.append(jnp.concatenate(tiles, axis=1))
    return jnp.concatenate(strips, axis=0)


def partial_kernel(edge, unit, first, hand_on, unroll, gm_hbm, um_hbm, gate, up, *rest):
    rest, (w, masks, sems, mask_sems) = rest[:-4], rest[-4:]
    *rest, tok_out = rest
    if hand_on:
        *rest, passed = rest
        passed[...] = rest[-3][...]
    *xs, pa, pb = rest if first else rest[1:]
    units = w.shape[2]
    starts = (unit * units, gate.shape[1] // 2 + unit * units)

    def mask_load(plane, src):
        return pltpu.make_async_copy(src, masks.at[plane], mask_sems.at[plane])

    def load(src, side, plane):
        slot = side * 2 + plane
        return pltpu.make_async_copy(src.at[:, pl.ds(starts[side], units)], w.at[slot], sems.at[slot])

    for plane, src in enumerate((gm_hbm, um_hbm)):
        mask_load(plane, src).start()
    for side in range(2):
        for plane, src in enumerate((gate, up)):
            load(src, side, plane).start()
    for plane, src in enumerate((gm_hbm, um_hbm)):
        mask_load(plane, src).wait()
    x = xs[0][...] if len(xs) == 1 else jnp.concatenate([part[...] for part in xs], axis=0)
    part = min(256, units)
    parts = units // part
    for side, out in enumerate((pa, pb)):
        def one(i, _, side=side, out=out):
            plane, n = i // parts, i % parts

            if isinstance(i, int):
                if n == 0:
                    load(gate, side, plane).wait()
                at = pl.ds(n * part, part)
            else:
                @pl.when(n == 0)
                def _():
                    load(gate, side, plane).wait()

                at = pl.ds(pl.multiple_of(n * part, part), part)
            col = starts[side] // edge + n * (part // edge)
            out[plane, :, at] = jnp.dot(
                x, masked(w[side * 2 + plane, :, at], lambda a, b: masks[plane, a, col + b], edge),
                preferred_element_type=jnp.float32,
            ).astype(out.dtype)
            return 0

        if unroll:
            for i in range(2 * parts):
                one(i, 0)
        else:
            lax.fori_loop(0, 2 * parts, one, 0)


def partials(tok, xs, gate, up, gm, um, unit, units, hand_on, unroll):
    rows, depth = xs[0].shape
    out = jax.ShapeDtypeStruct((2, rows * len(xs), units), jnp.bfloat16)
    first = tok is None
    return pl.pallas_call(
        functools.partial(partial_kernel, depth // gm.shape[0], unit, first, hand_on, unroll),
        in_specs=[ANY] * (4 if first else 5) + [VMEM] * len(xs),
        out_specs=[VMEM] * (3 if hand_on else 2) + [ANY],
        out_shape=[out, out] + [jax.ShapeDtypeStruct((rows, depth), jnp.bfloat16)] * hand_on + [TOKEN],
        scratch_shapes=[
            pltpu.VMEM((4, depth, units), jnp.bfloat16),
            pltpu.SMEM((2, *gm.shape), jnp.int32),
            pltpu.SemaphoreType.DMA((4,)),
            pltpu.SemaphoreType.DMA((2,)),
        ],
        input_output_aliases={} if first else {4: 3 if hand_on else 2},
        cost_estimate=LONG,
        compiler_params=pltpu.CompilerParams(vmem_limit_bytes=(46 if unroll else 48) * MIB),
    )(gm, um, gate, up, *([] if first else [tok]), *xs)


def swiglu(gate, up):
    return gate / (1.0 + jnp.exp(-gate)) * up


def over(rows, body):
    piece = min(16, rows)

    def one(i, _):
        body(pl.ds(pl.multiple_of(i * piece, piece), piece))
        return 0

    lax.fori_loop(0, rows // piece, one, 0)


def sum_kernel(own, n_col, goes_on, ends, z_ref, tok, left_in, right_in, *rest):
    n_own = len(own[0]) + len(own[1])
    mine, (*outs, tok_out, a, b, sems) = rest[:n_own], rest[n_own:]
    left_out, right_out = outs[:2] if goes_on else (None, None)
    z = z_ref[0]
    rows = a.shape[1]

    def each(act):
        for ref, (i, row), to, sem in zip(
            mine, own[0] + own[1], [a] * len(own[0]) + [b] * len(own[1]), [0] * len(own[0]) + [1] * len(own[1])
        ):
            @pl.when(z == i)
            def _(ref=ref, row=row, to=to, sem=sem):
                act(pltpu.make_async_copy(ref.at[:, pl.ds(row, rows), :], to, sems.at[sem]))

    each(lambda c: c.start())
    each(lambda c: c.wait())
    for side, came, here, goes, origin, end in (
        (0, left_in, a, left_out, n_col - 1, 0), (1, right_in, b, right_out, 0, n_col - 1)
    ):
        if goes_on:
            @pl.when(z == origin)
            def _(here=here, goes=goes):
                goes[...] = here[...]

            @pl.when((z != origin) & (z != end))
            def _(came=came, here=here, goes=goes):
                def add_up(r):
                    for p in range(2):
                        goes[p, r, :] = (came[p, r, :].astype(jnp.float32) + here[p, r, :].astype(jnp.float32)).astype(goes.dtype)
                over(rows, add_up)
        if ends:
            @pl.when(z == end)
            def _(side=side, came=came, here=here):
                def finish(r):
                    gate, up = (came[p, r, :].astype(jnp.float32) + here[p, r, :].astype(jnp.float32) for p in range(2))
                    outs[-1][side, r, :] = swiglu(gate, up).astype(outs[-1].dtype)
                over(rows, finish)


def sum_step(tok, z, left_in, right_in, own_a, own_b, goes_on, ends, n_col):
    _, rows, units = left_in.shape
    out = jax.ShapeDtypeStruct((2, rows, units), jnp.bfloat16)
    outs = [out] * (2 * goes_on + ends)
    own = (tuple(o[:2] for o in own_a), tuple(o[:2] for o in own_b))
    res = pl.pallas_call(
        functools.partial(sum_kernel, own, n_col, goes_on, ends),
        in_specs=[SMEM, ANY, VMEM, VMEM] + [ANY] * (len(own_a) + len(own_b)),
        out_specs=[VMEM] * len(outs) + [ANY],
        out_shape=outs + [TOKEN],
        scratch_shapes=[
            pltpu.VMEM((2, rows, units), jnp.bfloat16),
            pltpu.VMEM((2, rows, units), jnp.bfloat16),
            pltpu.SemaphoreType.DMA((2,)),
        ],
        input_output_aliases={1: len(outs)},
        cost_estimate=BRIEF,
        compiler_params=pltpu.CompilerParams(vmem_limit_bytes=8 * MIB),
    )(z, tok, left_in, right_in, *[o[2] for o in own_a], *[o[2] for o in own_b])
    sums = res[:2] if goes_on else (None, None)
    return sums, res[-2] if ends else None, res[-1]


def relay_kernel(n_col, made, got, z_ref, tok, *rest):
    fresh, rest = (rest[0], rest[1:]) if made else (None, rest)
    came, (left_out, right_out, tok_out) = rest[:-3], rest[-3:]
    z = z_ref[0]
    for side, out, end in ((0, right_out, 0), (1, left_out, n_col - 1)):
        if made:
            @pl.when(z == end)
            def _(side=side, out=out):
                out[...] = fresh[side]
        if got:
            @pl.when(z != end)
            def _(side=side, out=out):
                out[...] = came[side][...]


def relay(tok, z, fresh, came, n_col):
    like = came[0] if came else fresh
    out = jax.ShapeDtypeStruct(like.shape[-2:], jnp.bfloat16)
    made = fresh is not None
    return pl.pallas_call(
        functools.partial(relay_kernel, n_col, made, len(came) > 0),
        in_specs=[SMEM, ANY] + [VMEM] * (made + len(came)),
        out_specs=[VMEM, VMEM, ANY],
        out_shape=[out, out, TOKEN],
        input_output_aliases={1: 2},
        cost_estimate=LONG,
        compiler_params=pltpu.CompilerParams(vmem_limit_bytes=8 * MIB),
    )(z, tok, *([fresh] if made else []), *came)


def project_kernel(picks, edge, first, n_unit, blocks, more, last, unroll, z_ref, mask, tok, down, *rest):
    hidden, rest = rest[:len(picks)], rest[len(picks):]
    if more:
        total, rest = rest[0], rest[1:]
    outs, (tok_out, held, w, sems, w_sems) = rest[:-5], rest[-5:]
    z = z_ref[0]
    units = w.shape[1]
    count = held.shape[0] // 2
    rows = held.shape[1] // blocks
    slabs = 2
    wide = down.shape[1] // slabs
    thin = wide // 2

    def load(j, u, side):
        row = (side * n_unit + first + u) * units
        at = pl.ds(j * wide, wide)
        slot = side * count + u
        return pltpu.make_async_copy(
            down.at[pl.ds(row, units), at], w.at[slot, :, at], w_sems.at[j * (2 * count) + slot]
        )

    def every(act, j):
        for u in range(count):
            for side in range(2):
                act(load(j, u, side))

    for j in range(slabs):
        every(lambda c: c.start(), j)

    def each(act):
        for ref, (i, slot, block) in zip(hidden, picks):
            @pl.when(z == i)
            def _(ref=ref, slot=slot, block=block):
                act(pltpu.make_async_copy(
                    ref, held.at[slot, pl.ds(block * rows, rows), :], sems.at[slot * blocks + block]
                ))

    each(lambda c: c.start())
    each(lambda c: c.wait())

    def one(i, _):
        if unroll:
            if i % 2 == 0:
                every(lambda c: c.wait(), i // 2)
            at = pl.ds(i * thin, thin)
        else:
            for j in range(slabs):
                @pl.when(i == 2 * j)
                def _(j=j):
                    every(lambda c: c.wait(), j)

            at = pl.ds(pl.multiple_of(i * thin, thin), thin)
        terms = None
        for u in range(count):
            for side in range(2):
                slot = side * count + u
                row = (side * n_unit + first + u) * (units // edge)
                kept = masked(w[slot, :, at], lambda a, b: mask[row + a, i * (thin // edge) + b], edge)
                term = jnp.dot(held[slot], kept, preferred_element_type=jnp.float32)
                terms = term if terms is None else terms + term
        if more:
            terms = terms + total[:, at]
        if last:
            for k, out in enumerate(outs):
                out[:, at] = terms[k * rows:(k + 1) * rows, :].astype(out.dtype)
        else:
            outs[0][:, at] = terms
        return 0

    if unroll:
        for i in range(2 * slabs):
            one(i, 0)
    else:
        lax.fori_loop(0, 2 * slabs, one, 0)


def project(tok, z, hidden, down, mask, units, first, count, blocks, total, last, unroll):
    rows = hidden[0][3].shape[0]
    depth, width = down.shape
    edge = depth // mask.shape[0]
    n_unit = depth // 2 // units
    if last:
        out_shape = [jax.ShapeDtypeStruct((rows, width), jnp.bfloat16)] * blocks
    else:
        out_shape = [jax.ShapeDtypeStruct((blocks * rows, width), jnp.float32)]
    more = total is not None
    aliases = {2: len(out_shape)}
    if more and not last:
        aliases[4 + len(hidden)] = 0
    res = pl.pallas_call(
        functools.partial(project_kernel, tuple(h[:3] for h in hidden), edge, first, n_unit, blocks, more, last, unroll),
        in_specs=[SMEM, SMEM, ANY, pl.BlockSpec(memory_space=pltpu.HBM)] + [ANY] * len(hidden) + [VMEM] * more,
        out_specs=[VMEM] * len(out_shape) + [ANY],
        out_shape=out_shape + [TOKEN],
        scratch_shapes=[
            pltpu.VMEM((2 * count, blocks * rows, units), jnp.bfloat16),
            pltpu.VMEM((2 * count, units, width), jnp.bfloat16),
            pltpu.SemaphoreType.DMA((2 * count * blocks,)),
            pltpu.SemaphoreType.DMA((4 * count,)),
        ],
        input_output_aliases=aliases,
        cost_estimate=LONG,
        compiler_params=pltpu.CompilerParams(vmem_limit_bytes=46 * MIB),
    )(z, mask, tok, down, *[h[3] for h in hidden], *([total] if more else []))
    return res[:-1], res[-1]


def add_kernel(tok, x, y, out, tok_out):
    out[...] = (x[...].astype(jnp.float32) + y[...].astype(jnp.float32)).astype(out.dtype)


def add(tok, x, y):
    return pl.pallas_call(
        add_kernel,
        in_specs=[ANY, VMEM, VMEM],
        out_specs=[VMEM, ANY],
        out_shape=[jax.ShapeDtypeStruct(x.shape, x.dtype), TOKEN],
        input_output_aliases={0: 1},
        cost_estimate=BRIEF,
        compiler_params=pltpu.CompilerParams(vmem_limit_bytes=8 * MIB),
    )(tok, x, y)


def cycle(n_row, n_col):
    def at(r, i):
        return r * n_col + (n_col - 1 - i if r % 2 else i)

    steps = []
    for r in range(n_row):
        steps += [(at(r, i), at(r, i + 1)) for i in range(n_col - 1)] + [(at(r, n_col - 1), at(r ^ 1, 0))]
    return steps


def other(i, d, n_row):
    return (i // 2 + d // 2) % (n_row // 2) * 2 + (i % 2 ^ d % 2)


def pieces(group, n_unit):
    if n_unit % 2:
        return [(u, 1) for u in range(n_unit)]
    if group == [1] and n_unit > 2:
        return [(0, 1), (1, n_unit - 2), (n_unit - 1, 1)]
    halves = [(u, 2) for u in range(0, n_unit, 2)]
    return halves if group == [0] else halves[:-1] + [(n_unit - 2, 1), (n_unit - 1, 1)]


def shards(n_row, n_col, tokens, gate, up, down, gm, um, dm):
    half = gate.shape[1] // 2
    units = min(512, half)
    n_unit = half // units
    rows = tokens.shape[0]
    z, odd = lax.axis_index("col"), lax.axis_index("row") % 2
    z = jnp.where(odd == 1, n_col - 1 - z, z).astype(jnp.int32).reshape(1)
    to_right = cycle(n_row, n_col)
    to_left = [(j, i) for i, j in to_right]
    tok = None

    def swap(x, d, back=False):
        pairs = [(other(i, d, n_row), i) for i in range(n_row)]
        return lax.ppermute(x, "row", [(j, i) for i, j in pairs] if back else pairs)

    groups = [[0]] + [[d, d + 1] for d in range(2, n_row, 2)] + [[1]]
    xs = {0: tokens}
    chunks = [(d, u) for g in groups for u in range(n_unit) for d in g]
    n = len(chunks)
    first_end, last_end = n_col - 1, n + n_col - 2
    last_hop = last_end + n_col - 2
    own_a, own_b = {}, {}
    left_got, right_got, left_on, right_on, left_came, right_came = {}, {}, {}, {}, {}, {}

    def places(k):
        spots = []
        for i in range(n_col):
            t = k + first_end + i
            for side, at, on, came in ((0, i, right_on, right_came), (1, n_col - 1 - i, left_on, left_came)):
                spots.append((at, side, on[t] if t <= last_hop else came[t - 1]))
        return spots

    def compute(group, u):
        def run(tok):
            hand_on = group == [0] and u == min(1, n_unit - 1)
            pa, pb, *passed, tok = partials(tok, [xs[d] for d in group], gate, up, gm, um, u, units, hand_on, group != [0] or u > 1)
            if hand_on:
                for d in [*range(2, n_row), 1]:
                    xs[d] = swap(passed[0], d)
            for i, d in enumerate(group):
                k = chunks.index((d, u))
                own_a[k], own_b[k] = (i * rows, pa), (i * rows, pb)
            return tok
        return run

    totals, outs, pairs = {}, {}, []

    def down_projection(g, first, count):
        def run(tok):
            hidden = []
            for b, d in enumerate(g):
                for u in range(first, first + count):
                    for i, side, buf in places(chunks.index((d, u))):
                        hidden.append((i, side * count + u - first, b, buf))
            key, last = tuple(g), first + count == n_unit
            res, tok = project(tok, z, hidden, down, dm, units, first, count, len(g), totals.get(key), last, g == [1] and last)
            if last:
                outs.update(zip(g, res))
                if len(g) > 1:
                    pairs.append((g[0], swap(outs.pop(g[1]), 1)))
            else:
                totals[key] = res[0]
            return tok
        return run

    def add_pairs(tok):
        while pairs:
            d, theirs = pairs.pop()
            total, tok = add(tok, outs[d], theirs)
            outs[d] = swap(total, d, back=True)
        return tok

    work = {}
    for g in groups:
        for first, count in pieces(g, n_unit):
            k = max(chunks.index((d, u)) for d in g for u in range(first, first + count))
            work.setdefault(k + 2 * first_end, []).append(down_projection(g, first, count))
    needs = sorted((min(chunks.index((d, u)) for d in g), u, g) for g in groups for u in range(n_unit))
    for k, u, g in reversed(needs):
        at = next((s for s in range(k - 1, -1, -1) if s not in work), k - 1)
        work.setdefault(at, []).insert(0, compute(g, u))

    for run in work.get(-1, []):
        tok = run(tok)
    for t in range(last_hop + 2):
        fresh = None
        if t <= last_end:
            if t == 0:
                sums = own_a[0][1], own_b[0][1]
            else:
                mine_a = [(i, *own_a[t - (n_col - 1 - i)]) for i in range(n_col) if 0 <= t - (n_col - 1 - i) < n]
                mine_b = [(i, *own_b[t - i]) for i in range(n_col) if 0 <= t - i < n]
                sums, fresh, tok = sum_step(
                    tok, z, left_got[t - 1], right_got[t - 1], mine_a, mine_b, t < last_end, t >= first_end, n_col
                )
            if t < last_end:
                left_got[t] = lax.ppermute(sums[0], ("row", "col"), to_left)
                right_got[t] = lax.ppermute(sums[1], ("row", "col"), to_right)
        if first_end <= t <= last_hop:
            came = (right_came[t - 1], left_came[t - 1]) if t > first_end else ()
            left_on[t], right_on[t], tok = relay(tok, z, fresh, came, n_col)
            left_came[t] = lax.ppermute(left_on[t], ("row", "col"), to_left)
            right_came[t] = lax.ppermute(right_on[t], ("row", "col"), to_right)
        tok = add_pairs(tok)
        for run in work.get(t, []):
            tok = run(tok)
    tok = add_pairs(tok)

    mixed = sum(x.astype(jnp.float32) for d, x in outs.items() if d != 1)
    mixed = mixed + swap(outs[1], 1).astype(jnp.float32)
    return mixed.astype(jnp.bfloat16)


def solution(mesh):
    in_specs = (
        P(("groups", "row"), "col"),
        P("col", "row"),
        P("col", "row"),
        P("row", "col"),
        P("col", "row"),
        P("col", "row"),
        P("row", "col"),
    )
    out_specs = P(("groups", "row"), "col")
    body = functools.partial(shards, mesh.shape["row"], mesh.shape["col"])
    return jax.shard_map(body, mesh=mesh, in_specs=in_specs, out_specs=out_specs, check_vma=False)
```
